32 devices in a mesh: row: 4 (over y, x), col: 4 (over z), seq: 2 (over core).
Axes of the slice: x: 2, y: 2, z: 4, core: 2. Of those that a mesh axis runs over, the one named last changes fastest.
Arguments:
- alignment_tensor: bfloat16 [256, 128, 256], P('seq', ('row', 'col')), may hold values from -6 to 6
- occupancy_matrix: int32 [256, 128], P(None, ('row', 'col')), may hold values from 0 to 1, as said below
- first_factor_matrix: bfloat16 [256, 32], replicated, may hold values from -0.375 to 0.375
- second_factor_matrix: bfloat16 [256, 32], replicated, may hold values from -0.375 to 0.375
- couple_factor_matrix: bfloat16 [1024, 128], replicated, may hold values from -3 to 3
- couple_increment_adjoint: bfloat16 [128, 128, 128], P(('row', 'seq'), 'col'), may hold values from -6 to 6
Outputs:
- couple_increment: bfloat16 [128, 128, 128], P(('row', 'seq'), 'col')
- alignment_adjoint: bfloat16 [256, 128, 256], P('seq', ('row', 'col'))
- first_factor_adjoint: float32 [256, 32], replicated
- second_factor_adjoint: float32 [256, 32], replicated
- couple_factor_adjoint: float32 [1024, 128], replicated
The draws below stay inside these ranges and needn't reach their ends.
Inputs may be any that keep to these rules, and one draw needn't show every extreme that they name: Row 0 of occupancy_matrix (the query) is all ones; every other sequence covers residues of one contiguous range with some gaps.
All inputs are finite; a program needn't handle non-finite values.
Results may differ from the reference program's by a relative error of at most 0.0076.
Values may be sent and summed in bfloat16 or wider, within the bound.
No kernel may reach another device: no remote copies, remote signals or barrier semaphores. Data moves between devices by JAX's collectives and lax.ppermute only.
A program may use at most 192 MiB of HBM per device.

```python
import jax
import jax.numpy as jnp
from jax import lax

ALIGN_DIM = 256
PROJ_DIM = 32
CZ = 128
OUTER = 1024
Q = 8
NUM_HOMOLOGS = 256
NUM_AMINO = 128
N_COL = 4


def draw_occupancy_matrix(key, part):
    key = jax.random.fold_in(key, 7)
    key_start, key_length, key_keep = jax.random.split(key, 3)
    starts = jax.random.randint(key_start, (NUM_HOMOLOGS, 1), 0, NUM_AMINO)
    spans = jax.random.randint(key_length, (NUM_HOMOLOGS, 1), NUM_AMINO // 8, NUM_AMINO + 1)
    places = jnp.arange(NUM_AMINO, dtype=jnp.int32)[None, :]
    inside = (places >= starts) & (places < starts + spans)
    kept = jax.random.randint(key_keep, (NUM_HOMOLOGS, NUM_AMINO), 0, 100) < 85
    argument_tensor = (inside & kept).astype(jnp.int32)
    first = jnp.arange(NUM_HOMOLOGS, dtype=jnp.int32)[:, None] == 0
    return jnp.where(first, jnp.ones_like(argument_tensor), argument_tensor)


def steps_of(stream_key, shape, pieces, low, largest):
    loudness, own = 1.0, jax.random.fold_in(stream_key, 6)
    for dim, shards_of in pieces:
        draws = jnp.exp(jax.random.uniform(jax.random.fold_in(own, dim), (shards_of,), jnp.float32, low / len(pieces), largest / len(pieces)))
        loudness = loudness * jnp.repeat(draws, shape[dim] // shards_of).reshape([-1 if axis == dim else 1 for axis in range(len(shape))])
    return loudness


def centred(rng, extent, deviation, most, cuts=(), held_as=jnp.bfloat16):
    factor_of = steps_of(rng, extent, cuts, -0.22, 0.18) if cuts else 1.0
    drawn = jax.random.normal(rng, extent, jnp.float32) * deviation * factor_of
    return jnp.minimum(jnp.maximum(drawn, -most), most).astype(held_as)


def setup_inputs(seed: int = 0) -> dict:
    key_of = jax.random.split(jax.random.key(seed), 7)
    alignment_tensor = centred(key_of[0], (NUM_HOMOLOGS, NUM_AMINO, ALIGN_DIM), 1.0, 6.0, ((0, 2), (1, 16)))
    occupancy_matrix = draw_occupancy_matrix(jax.random.fold_in(key_of[6], 71), 0)
    first_factor_matrix = centred(key_of[2], (ALIGN_DIM, PROJ_DIM), ALIGN_DIM ** -0.5, 0.375)
    second_factor_matrix = centred(key_of[3], (ALIGN_DIM, PROJ_DIM), ALIGN_DIM ** -0.5, 0.375)
    couple_factor_matrix = centred(key_of[4], (OUTER, CZ), 0.5, 3.0)
    couple_increment_adjoint = centred(key_of[5], (NUM_AMINO, NUM_AMINO, CZ), 1.0, 6.0, ((0, 8), (1, 4)))
    return dict(alignment_tensor=alignment_tensor, occupancy_matrix=occupancy_matrix, first_factor_matrix=first_factor_matrix, second_factor_matrix=second_factor_matrix, couple_factor_matrix=couple_factor_matrix, couple_increment_adjoint=couple_increment_adjoint)


def apply_norming(alignment_tensor):
    argument_tensor = alignment_tensor.astype(jnp.float32)
    centered_input = argument_tensor - lax.optimization_barrier(jnp.mean(argument_tensor, axis=-1, keepdims=True))
    reciprocal_spread = lax.rsqrt(lax.optimization_barrier(jnp.mean(centered_input * centered_input, axis=-1, keepdims=True)) + 1e-05)
    return (centered_input * reciprocal_spread, reciprocal_spread)

def reference(alignment_tensor, occupancy_matrix, first_factor_matrix, second_factor_matrix, couple_factor_matrix, couple_increment_adjoint):
    homolog_rows, amino_positions = occupancy_matrix.shape
    block = Q * N_COL
    nblocks = amino_positions // block
    zscored_tensor, reciprocal_spread = apply_norming(alignment_tensor)
    rescaled_tensor = zscored_tensor.astype(jnp.bfloat16)
    maskf = occupancy_matrix.astype(jnp.float32)
    raveled_matrix = rescaled_tensor.reshape(-1, ALIGN_DIM)
    left = (maskf[:, :, None] * jnp.dot(raveled_matrix, first_factor_matrix, preferred_element_type=jnp.float32).reshape(homolog_rows, amino_positions, PROJ_DIM)).astype(jnp.bfloat16)
    right = (maskf[:, :, None] * jnp.dot(raveled_matrix, second_factor_matrix, preferred_element_type=jnp.float32).reshape(homolog_rows, amino_positions, PROJ_DIM)).astype(jnp.bfloat16)
    count = jnp.dot(maskf.T, maskf, precision=lax.Precision.HIGHEST)
    den = count + 0.001
    right32 = right.astype(jnp.float32)
    wo32 = couple_factor_matrix.astype(jnp.float32)

    def outer_of(index):
        lblock = lax.dynamic_slice_in_dim(left, index * block, block, 1).astype(jnp.float32)
        outer = jnp.einsum('sic,sje->ijce', lblock, right32).reshape(block, amino_positions, PROJ_DIM * PROJ_DIM)
        return (outer, lblock)

    def forward(index):
        outer, lblock = outer_of(index)
        value = jnp.dot(outer.reshape(-1, PROJ_DIM * PROJ_DIM), wo32, precision=lax.Precision.HIGHEST).reshape(block, amino_positions, CZ)
        dblock = lax.dynamic_slice_in_dim(den, index * block, block, 0)
        return (value / dblock[:, :, None]).astype(jnp.bfloat16)
    indexes = jnp.arange(nblocks, dtype=jnp.int32)
    couple_increment = lax.map(forward, indexes).reshape(amino_positions, amino_positions, CZ)

    def backward(carry, index):
        g_right, d_wo = carry
        outer, lblock = outer_of(index)
        dblock = lax.dynamic_slice_in_dim(den, index * block, block, 0)
        gblock = lax.dynamic_slice_in_dim(couple_increment_adjoint, index * block, block, 0).astype(jnp.float32)
        scaled = (gblock / dblock[:, :, None]).astype(jnp.bfloat16)
        d_outer = jnp.dot(scaled.reshape(-1, CZ), couple_factor_matrix.T, preferred_element_type=jnp.float32).astype(jnp.bfloat16)
        d_outer = d_outer.reshape(block, amino_positions, PROJ_DIM, PROJ_DIM).astype(jnp.float32)
        g_lblock = jnp.einsum('ijce,sje->sic', d_outer, right32)
        g_right = g_right + jnp.einsum('ijce,sic->sje', d_outer, lblock)
        d_wo = d_wo + jnp.dot(outer.reshape(-1, PROJ_DIM * PROJ_DIM).T, scaled.astype(jnp.float32).reshape(-1, CZ), precision=lax.Precision.HIGHEST)
        return ((g_right, d_wo), g_lblock)
    start = (jnp.zeros((homolog_rows, amino_positions, PROJ_DIM), jnp.float32), jnp.zeros((PROJ_DIM * PROJ_DIM, CZ), jnp.float32))
    (g_right, couple_factor_adjoint), g_blocks = lax.scan(backward, start, indexes)
    g_left = jnp.transpose(g_blocks, (1, 0, 2, 3)).reshape(homolog_rows, amino_positions, PROJ_DIM)
    g_left = maskf[:, :, None] * g_left
    g_right = maskf[:, :, None] * g_right
    gl_flat = g_left.reshape(-1, PROJ_DIM)
    gr_flat = g_right.reshape(-1, PROJ_DIM)
    normed32 = raveled_matrix.astype(jnp.float32)
    first_factor_adjoint = jnp.dot(normed32.T, gl_flat, precision=lax.Precision.HIGHEST)
    second_factor_adjoint = jnp.dot(normed32.T, gr_flat, precision=lax.Precision.HIGHEST)
    rescaled_adjoint = jnp.dot(gl_flat, first_factor_matrix.astype(jnp.float32).T, precision=lax.Precision.HIGHEST)
    rescaled_adjoint = rescaled_adjoint + jnp.dot(gr_flat, second_factor_matrix.astype(jnp.float32).T, precision=lax.Precision.HIGHEST)
    rescaled_adjoint = rescaled_adjoint.reshape(homolog_rows, amino_positions, ALIGN_DIM)
    addend_term = lax.optimization_barrier(jnp.mean(rescaled_adjoint * zscored_tensor, axis=-1, keepdims=True))
    alignment_adjoint = (reciprocal_spread * (rescaled_adjoint - lax.optimization_barrier(jnp.mean(rescaled_adjoint, axis=-1, keepdims=True)) - zscored_tensor * addend_term)).astype(jnp.bfloat16)
    return (couple_increment, alignment_adjoint, first_factor_adjoint, second_factor_adjoint, couple_factor_adjoint)
```

```python
import functools
import math

import jax
import jax.numpy as jnp
from jax import lax
from jax.experimental import pallas as pl
from jax.experimental.pallas import tpu as pltpu
from jax.sharding import PartitionSpec as P

ALIGN = 256
PROJ = 32
CZ = 128
OUTER = 1024
PAD = 16
AXES = ("row", "col", "seq")
BF = jnp.bfloat16
F32 = jnp.float32

NN = (((1,), (0,)), ((), ()))
NT = (((1,), (1,)), ((), ()))
TN = (((0,), (0,)), ((), ()))


def dot(a, b, dims):
    return lax.dot_general(a, b, dims, preferred_element_type=F32)


def normalize(x):
    centered = x - jnp.mean(x, axis=-1, keepdims=True)
    rstd = lax.rsqrt(jnp.mean(centered * centered, axis=-1, keepdims=True) + 1e-05)
    return centered * rstd, rstd


def strided(ref, place):
    return jnp.concatenate([ref[0, place, :], ref[1, place, :]], axis=1)


def own_mask(mask_ref, seqs):
    start = pl.multiple_of(lax.axis_index("seq") * seqs, seqs)
    return mask_ref[:, pl.ds(start, seqs)].astype(F32)


def norm_kernel(x_ref, normed_ref, token_ref, rows):
    q, seqs, _ = normed_ref.shape
    xhat = normalize(x_ref[...].astype(F32))[0]
    rows[0], rows[1] = xhat[:, :128], xhat[:, 128:]
    for i in range(q):
        normed_ref[i] = strided(rows, pl.ds(i, seqs, stride=q)).astype(BF)
    token_ref[...] = jnp.zeros_like(token_ref)


def copy_all(pairs, sems):
    copies = [pltpu.make_async_copy(a, b, sems.at[k]) for k, (a, b) in enumerate(pairs)]
    for copy in copies:
        copy.start()
    return copies


def project_kernel(
    x_hbm, mask_hbm, wl_hbm, wr_hbm, adj_hbm,
    right_hbm, *refs
):
    *col_hbm, x_ref, mask_ref, wl_ref, wr_ref, adj_ref, right_ref, left_ref, pairs_ref, rows, spread, sems = refs
    q, seqs = mask_ref.shape[0], right_ref.shape[1]
    n_col = len(col_hbm)
    col = lax.axis_index("col")
    chunk = q * PROJ
    held = ((adj_hbm, adj_ref), (x_hbm, x_ref), (mask_hbm, mask_ref), (wl_hbm, wl_ref), (wr_hbm, wr_ref))
    loads = copy_all(held, sems)
    loads[0].wait()
    pairs = adj_ref[...].astype(F32).reshape(-1, n_col, q, CZ)
    for p in range(n_col):
        pairs_ref[p] = pairs[:, p].reshape(-1, CZ).astype(BF)
    place, rest = pl.ds(0, chunk + PAD), pl.ds(chunk + PAD, pairs_ref.shape[1])
    sent = copy_all(
        [(pairs_ref.at[col ^ k], hbm.at[rest, :]) for k, hbm in enumerate(col_hbm)],
        sems.at[pl.ds(6 + n_col, n_col)],
    )
    for copy in loads[1:]:
        copy.wait()
    xhat = normalize(x_ref[...].astype(F32))[0]
    rows[0], rows[1] = xhat[:, :128], xhat[:, 128:]
    mask = own_mask(mask_ref, seqs)
    weights = jnp.concatenate([wl_ref[...], wr_ref[...]], axis=0)
    for i in range(q):
        mine = strided(rows, pl.ds(i, seqs, stride=q)).astype(BF)
        both = dot(weights, mine, NT) * mask[i : i + 1, :]
        left_ref[i * PROJ : (i + 1) * PROJ, :] = both[:PROJ].astype(BF)
        spread[pl.ds(i, PROJ, stride=q), :] = both[PROJ:]
    whole = mask_ref[...].astype(F32)
    halves = [whole[:, t * seqs : (t + 1) * seqs] for t in range(whole.shape[1] // seqs)]
    tail = jnp.concatenate(halves, axis=0).astype(BF)
    left_ref[chunk:, :] = tail
    right_ref[...] = jnp.concatenate([spread[...].astype(BF), tail], axis=0)
    sent += copy_all(
        [(right_ref, right_hbm)]
        + [(left_ref, hbm.at[place, :]) for hbm in col_hbm],
        sems.at[pl.ds(5, n_col + 1)],
    )
    for copy in sent:
        copy.wait()


def far_first(count):
    return sorted(range(count), key=lambda k: (k & 2) == 0)


def by_partner(refs):
    return [refs[far_first(len(refs)).index(k)] for k in range(len(refs))]


def sent_order(values):
    return [values[k] for k in far_first(len(values))]


def unpack_mask(tail, q):
    tail = tail.astype(F32)
    return jnp.concatenate([tail[t * q : (t + 1) * q] for t in range(tail.shape[0] // q)], axis=1)


def pack_kernel(n_row, ready_ref, *refs):
    *ins, mine_ref, theirs_ref, mask_right, mask_left, adj_ref, left_ref, masks_ref = refs
    cols, rights = ins[:-n_row][::-1], ins[-n_row:]
    half, chunk = len(cols) // 2, mine_ref.shape[1]
    size, q = chunk + PAD, mask_right.shape[0] // n_row
    row, col, seq = (lax.axis_index(name) for name in AXES)
    for k, ref in enumerate(rights):
        mine_ref[row ^ k] = ref[:chunk, :]
        theirs_ref[row ^ k] = ref[:chunk, :]
        mask_right[pl.ds(pl.multiple_of((row ^ k) * q, q), q), :] = unpack_mask(ref[chunk:, :], q)
    for k, ref in enumerate(cols):
        left_ref[col ^ k] = ref[:chunk, :]
        masks_ref[col ^ k] = unpack_mask(ref[chunk:size, :], q)
        adj_ref[col ^ k] = ref[size:, :]
    for k in range(half):
        mine_ref[n_row + k] = left_ref[seq * half + k]
        theirs_ref[n_row + k] = left_ref[(1 - seq) * half + k]
        mask_left[k * q : (k + 1) * q, :] = masks_ref[seq * half + k]


def exchange(blocks):
    lane = lax.broadcasted_iota(jnp.int32, blocks[0].shape, 1)
    even = (lane & 32) == 0
    low = lane < 64
    a = list(blocks)
    for p in (0, 2):
        first, second = a[p], a[p + 1]
        a[p] = jnp.where(even, first, pltpu.roll(second, 32, 1))
        a[p + 1] = jnp.where(even, pltpu.roll(first, 96, 1), second)
    for p in (0, 1):
        first, second = a[p], a[p + 2]
        a[p] = jnp.where(low, first, pltpu.roll(second, 64, 1))
        a[p + 2] = jnp.where(low, pltpu.roll(first, 64, 1), second)
    return a


def back_kernel(
    wp, mr, ml, adj_ref, mine, dd, scaled_ref, recip_ref, rt_ref, d3
):
    n_col, pairs, _ = adj_ref.shape
    rows_i, depth = ml.shape
    rows_j, q = mr.shape[0], pairs // rows_i
    mask_r = mr[...]
    both = jnp.concatenate([(ml[i : i + 1, :] * mask_r).astype(BF) for i in range(rows_i)], axis=0)
    count = dot(both, jnp.ones((depth, CZ), BF), NN)
    recip = 1.0 / (count + 0.001)
    recip_ref[...] = recip
    adjoint = jnp.stack(
        [adj_ref[p].astype(F32).reshape(rows_i, q, CZ) for p in range(n_col)], axis=1
    ).reshape(rows_i * rows_j, CZ)
    scaled = (adjoint * recip).astype(BF)
    scaled_ref[...] = scaled.astype(F32).T.astype(BF)
    rt_ref[...] = by_channel(mine, mr.shape[0] // q, q)
    d3[...] = dot(scaled, wp[...], NT)
    for g in range(PROJ // 4):
        for ig in range(rows_i // 4):
            blocks = [
                d3[(ig * 4 + b) * rows_j : (ig * 4 + b + 1) * rows_j, g * 128 : (g + 1) * 128]
                for b in range(4)
            ]
            for e, value in enumerate(exchange(blocks)):
                row = (g * 4 + e) * rows_j
                dd[row : row + rows_j, ig * 128 : (ig + 1) * 128] = value.astype(BF)


def by_channel(packed, n_row, q):
    blocks = [packed[r].astype(F32).reshape(PROJ, q, -1) for r in range(n_row)]
    return jnp.concatenate(blocks, axis=1).reshape(PROJ * n_row * q, -1).astype(BF)


def left_kernel(rt_mine, theirs, dd, rt, mine_ref, theirs_ref, parts):
    half, chunk, seqs = mine_ref.shape
    n_row, q = theirs.shape[0] - half, chunk // PROJ
    seq = lax.axis_index("seq")
    rt[:, pl.ds(pl.multiple_of(seq * seqs, seqs), seqs)] = rt_mine[...]
    rt[:, pl.ds(pl.multiple_of((1 - seq) * seqs, seqs), seqs)] = by_channel(theirs, n_row, q)
    g_left = dot(dd[...], rt[...], TN)
    for t in range(2):
        for k in range(half):
            part = g_left[k * chunk : (k + 1) * chunk, t * seqs : (t + 1) * seqs]
            parts[t, k] = part.astype(BF)
    mine_ref[...] = parts[seq]
    theirs_ref[...] = parts[1 - seq]


def pair_kernel(
    rt, wp, dd, scaled_ref, recip_ref, mine, theirs,
    mine_ref, theirs_ref, couple_ref,
    lt, wf, o3, parts,
):
    n_col, pairs, _ = couple_ref.shape
    _, chunk, seqs = mine.shape
    q = chunk // PROJ
    half = n_col // 2
    rows_i = half * q
    rows_j = dd.shape[0] // PROJ
    n_row = rows_j // q
    depth = rt.shape[1]
    seq = lax.axis_index("seq")
    for ref, side in ((mine, seq), (theirs, 1 - seq)):
        lanes = pl.ds(pl.multiple_of(side * seqs, seqs), seqs)
        for k in range(half):
            lt[k * chunk : (k + 1) * chunk, lanes] = ref[n_row + k]
    for g in range(PROJ // 4):
        part = dot(rt[g * 4 * rows_j : (g + 1) * 4 * rows_j, :], lt[...], NT)
        for ig in range(rows_i // 4):
            lanes = slice(ig * 128, (ig + 1) * 128)
            blocks = [part[e * rows_j : (e + 1) * rows_j, lanes] for e in range(4)]
            for b, value in enumerate(exchange(blocks)):
                i = ig * 4 + b
                o3[i * rows_j : (i + 1) * rows_j, g * 128 : (g + 1) * 128] = value.astype(BF)
    couple = (dot(o3[...], wp[...], NN) * recip_ref[...]).reshape(rows_i, n_col, q, CZ)
    for p in range(n_col):
        couple_ref[p] = couple[:, p].reshape(pairs, CZ).astype(BF)
    dwo = dot(scaled_ref[...], o3[...], NN).T
    for e in range(PROJ):
        wf[pl.ds(e, PROJ, stride=PROJ), :] = dwo[e * PROJ : (e + 1) * PROJ, :]
    split = OUTER // 2 // chunk
    g_right = dot(dd[...], lt[...], NN).reshape(PROJ, rows_j, depth)
    for t in range(2):
        lanes = slice(t * seqs, (t + 1) * seqs)
        for r in range(n_row):
            parts[t, r] = g_right[:, r * q : (r + 1) * q, lanes].reshape(chunk, seqs).astype(BF)
        for k in range(split):
            row = (t * split + k) * chunk
            parts[t, n_row + k] = wf[row : row + chunk, :].astype(BF)
    mine_ref[...] = parts[seq]
    theirs_ref[...] = parts[1 - seq]


def merge_left_kernel(mine_ref, got_ref, couple_ref, held_ref, passed_ref, *refs):
    *outs, left_ref = refs
    passed_ref[...] = held_ref[...]
    half, chunk, _ = mine_ref.shape
    col, seq = lax.axis_index("col"), lax.axis_index("seq")
    for k in range(half):
        left_ref[seq * half + k] = mine_ref[k]
        left_ref[(1 - seq) * half + k] = got_ref[k]
    for k, ref in enumerate(outs):
        ref[:chunk, :] = left_ref[col ^ k]
        ref[chunk:, :] = couple_ref[col ^ k]


def merge_right_kernel(mine_ref, got_ref, *refs):
    *outs, dwo_ref = refs
    n_row, chunk = len(outs), mine_ref.shape[1]
    row = lax.axis_index("row")
    dwo = mine_ref[n_row:].astype(F32) + got_ref[n_row:].astype(F32)
    dwo_ref[...] = dwo.astype(BF).reshape(dwo_ref.shape)
    for k, ref in enumerate(outs):
        ref[:chunk, :] = (mine_ref[row ^ k].astype(F32) + got_ref[row ^ k].astype(F32)).astype(BF)
        ref[chunk:, :] = dwo_ref[row ^ k]


def add_all(refs):
    return functools.reduce(lambda a, b: a + b, [ref[...].astype(F32) for ref in refs])


def weights_kernel(n_row, n_col, normed_ref, mask_ref, *refs):
    col_refs, row_refs = refs[:n_col][::-1], refs[n_col : n_row + n_col][::-1]
    pay_ref, parts_ref, couple_ref, spread = refs[n_row + n_col :]
    q, seqs, _ = normed_ref.shape
    chunk = q * PROJ
    mask = own_mask(mask_ref, seqs)
    g_left = add_all([ref.at[:chunk, :] for ref in col_refs])
    g_right = add_all([ref.at[:chunk, :] for ref in row_refs])
    pay_ref[4 * PROJ :, :] = add_all([ref.at[chunk:, :] for ref in row_refs]).astype(BF)
    spread[...] = (g_right.reshape(PROJ, q, seqs) * mask[None]).reshape(chunk, seqs)
    total = jnp.zeros((4 * PROJ, ALIGN), F32)
    for i in range(q):
        left = g_left[i * PROJ : (i + 1) * PROJ] * mask[i : i + 1, :]
        g = jnp.concatenate([left, spread[pl.ds(i, PROJ, stride=q), :]], axis=0)
        high = g.astype(BF).astype(F32)
        parts = jnp.concatenate([high, g - high], axis=0).astype(BF)
        parts_ref[i] = parts
        total = total + dot(parts, normed_ref[i], NN)
    d_weights = total[: 2 * PROJ] + total[2 * PROJ :]
    pay_ref[: 2 * PROJ, :] = d_weights[:, :128].astype(BF)
    pay_ref[2 * PROJ : 4 * PROJ, :] = d_weights[:, 128:].astype(BF)
    for k, ref in enumerate(col_refs):
        couple_ref[lax.axis_index("col") ^ k] = ref[chunk:, :]


def hold_kernel(right_ref, left_ref, w_ref, right_out, left_out, wp_ref, wf):
    right_out[...] = right_ref[...]
    left_out[...] = left_ref[...]
    wf[...] = w_ref[...].astype(F32)
    for e in range(PROJ):
        wp_ref[e * PROJ : (e + 1) * PROJ, :] = wf[pl.ds(e, PROJ, stride=PROJ), :].astype(BF)


def input_kernel(x_ref, wl_ref, wr_ref, parts_ref, dx_ref, token_ref, rows):
    q, _, seqs = parts_ref.shape
    weights = jnp.concatenate([wl_ref[...], wr_ref[...]] * 2, axis=0)
    for i in range(q):
        d_rows = dot(parts_ref[i], weights, TN)
        rows[0, pl.ds(i, seqs, stride=q), :] = d_rows[:, :128]
        rows[1, pl.ds(i, seqs, stride=q), :] = d_rows[:, 128:]
    xhat, rstd = normalize(x_ref[...].astype(F32))
    d_normed = strided(rows, slice(None))
    along = jnp.mean(d_normed * xhat, axis=-1, keepdims=True)
    dx = rstd * (d_normed - jnp.mean(d_normed, axis=-1, keepdims=True) - xhat * along)
    dx_ref[...] = dx.astype(BF)
    token_ref[...] = jnp.zeros_like(token_ref)


def place_kernel(q, couple_ref, out_ref, token_ref):
    pieces = [couple_ref[p].astype(F32).reshape(-1, q, CZ) for p in range(couple_ref.shape[0])]
    out_ref[...] = jnp.stack(pieces, axis=1).reshape(-1, CZ).astype(BF)
    token_ref[...] = jnp.zeros_like(token_ref)


def sum_kernel(axis, size, *refs):
    out_ref, held = refs[-2:]
    for k, ref in enumerate(by_partner(refs[:size])):
        held[lax.axis_index(axis) ^ k] = ref[...]
    out_ref[...] = add_all([held.at[k] for k in range(size)]).astype(BF)


def join_kernel(axis, size, *refs):
    ins = refs[:size][::-1]
    out_ref, sums, runs = refs[-3:]
    head = 4 * PROJ
    rows = ins[0].shape[0] - head
    for k, ref in enumerate(ins):
        place = lax.axis_index(axis) ^ k
        sums[place] = ref[:head, :]
        runs[pl.ds(pl.multiple_of(place * rows, rows), rows), :] = ref[head:, :].astype(F32)
    out_ref[:head, :] = add_all([sums.at[k] for k in range(size)]).astype(BF)
    out_ref[head:, :] = runs[...].astype(BF)


def total_kernel(mine_ref, theirs_ref, first_ref, second_ref, dwo_ref):
    head = 4 * PROJ
    seq = lax.axis_index("seq")
    for ref, side in ((mine_ref, seq), (theirs_ref, 1 - seq)):
        start = pl.multiple_of(side * (OUTER // 2), OUTER // 2)
        dwo_ref[pl.ds(start, OUTER // 2), :] = ref[head:, :].astype(F32)
    total = mine_ref[:head, :].astype(F32) + theirs_ref[:head, :].astype(F32)
    first_ref[:, :128] = total[:PROJ]
    first_ref[:, 128:] = total[2 * PROJ : 3 * PROJ]
    second_ref[:, :128] = total[PROJ : 2 * PROJ]
    second_ref[:, 128:] = total[3 * PROJ :]


def params(mib):
    return pltpu.CompilerParams(vmem_limit_bytes=mib * 1024 * 1024)


def shape(*dims, dtype=BF):
    return jax.ShapeDtypeStruct(dims, dtype)


def call(kernel, name, inputs, outputs, scratch=(), hbm_in=0, hbm_out=0, sems=0, mib=None, cost=None):
    def specs(count, hbm):
        return [pl.BlockSpec(memory_space=pltpu.HBM if k < hbm else pltpu.VMEM) for k in range(count)]

    held = sum(2 * math.prod(dims) for dims, _ in scratch)
    buffers = [pltpu.VMEM(dims, dtype) for dims, dtype in scratch]
    if sems:
        buffers.append(pltpu.SemaphoreType.DMA((sems,)))
    return pl.pallas_call(
        kernel,
        out_shape=outputs,
        in_specs=specs(len(inputs), hbm_in),
        out_specs=tuple(specs(len(outputs), hbm_out)),
        scratch_shapes=buffers,
        compiler_params=params(mib or 16 + 2 * held // 1024**2),
        cost_estimate=cost and pl.CostEstimate(flops=cost[0], bytes_accessed=cost[1], transcendentals=0),
        name=name,
    )(*inputs)


def local(n_row, n_col, n_seq, x, occupancy, first, second, couple, adjoint):
    seqs, q, _ = x.shape
    rows_i, rows_j, _ = adjoint.shape
    half = n_col // n_seq
    chunk = q * PROJ
    depth = seqs * n_seq
    pairs = rows_i * q
    flat = x.reshape(seqs * q, ALIGN)
    mask = occupancy.T
    wl, wr = first.T, second.T

    right, *lefts = call(
        project_kernel,
        "project",
        (flat, mask, wl, wr, adjoint.reshape(rows_i * rows_j, CZ)),
        (
            shape(chunk + PAD, seqs),
            *[shape(chunk + PAD + pairs, seqs)] * n_col,
        ),
        [
            ((seqs * q, ALIGN), BF),
            ((q, depth), jnp.int32),
            ((PROJ, ALIGN), BF),
            ((PROJ, ALIGN), BF),
            ((rows_i * rows_j, CZ), BF),
            ((chunk + PAD, seqs), BF),
            ((chunk + PAD, seqs), BF),
            ((n_col, pairs, CZ), BF),
            ((2, seqs * q, ALIGN // 2), F32),
            ((chunk, seqs), F32),
        ],
        hbm_in=5,
        hbm_out=1 + n_col,
        sems=6 + 2 * n_col,
        mib=60,
    )

    def partner(value, axis, k):
        size = {"row": n_row, "col": n_col, "seq": n_seq}[axis]
        return lax.ppermute(value, axis, [(d, d ^ k) for d in range(size)])

    def spread(values, axis):
        return [values[0]] + [partner(values[k], axis, k) for k in range(1, len(values))]

    held, left, wp = call(
        hold_kernel,
        "hold",
        (right, lefts[0], couple),
        (shape(*right.shape), shape(*lefts[0].shape), shape(OUTER, CZ)),
        [((OUTER, CZ), F32)],
        cost=(2**20, 2**20),
    )
    rights = [held] + spread([right] * n_row, "row")[1:]
    lefts = [left] + spread(lefts, "col")[1:]
    normed, ready = call(
        norm_kernel,
        "norm",
        (flat,),
        (shape(q, seqs, ALIGN), shape(8, CZ, dtype=F32)),
        [((2, seqs * q, ALIGN // 2), F32)],
        cost=(2**28, 2**21),
    )
    count = n_row + half
    mine, theirs, mask_right, mask_left, adjoints = call(
        functools.partial(pack_kernel, n_row),
        "pack",
        (ready, *lefts[::-1], *rights),
        (
            shape(count, chunk, seqs),
            shape(count, chunk, seqs),
            shape(rows_j, depth, dtype=F32),
            shape(rows_i, depth, dtype=F32),
            shape(n_col, pairs, CZ),
        ),
        [((n_col, chunk, seqs), BF), ((n_col, q, depth), F32)],
    )
    theirs = partner(theirs, "seq", 1)
    dd, scaled, recip, rt_mine = call(
        back_kernel,
        "back",
        (wp, mask_right, mask_left, adjoints, mine),
        (
            shape(PROJ * rows_j, rows_i * PROJ),
            shape(CZ, rows_i * rows_j),
            shape(rows_i * rows_j, CZ, dtype=F32),
            shape(PROJ * rows_j, seqs),
        ),
        [((rows_i * rows_j, OUTER), F32)],
        cost=(2**30, 2**23),
    )
    rt, left_mine, left_theirs = call(
        left_kernel,
        "left",
        (rt_mine, theirs, dd),
        (shape(PROJ * rows_j, depth), shape(half, chunk, seqs), shape(half, chunk, seqs)),
        [((2, half, chunk, seqs), BF)],
        cost=(2**30, 2**23),
    )
    got = partner(left_theirs, "seq", 1)
    parts = n_row + OUTER // 2 // chunk
    right_mine, right_theirs, pieces = call(
        pair_kernel,
        "pair",
        (rt, wp, dd, scaled, recip, mine, theirs),
        (
            shape(parts, chunk, seqs),
            shape(parts, chunk, seqs),
            shape(n_col, pairs, CZ),
        ),
        [
            ((rows_i * PROJ, depth), BF),
            ((OUTER, CZ), F32),
            ((rows_i * rows_j, OUTER), BF),
            ((2, parts, chunk, seqs), BF),
        ],
        cost=(2**30, 2**23),
    )
    piece = OUTER // 2 // n_row
    right_theirs, *lefts = call(
        merge_left_kernel,
        "merge_left",
        (left_mine, got, pieces, right_theirs),
        [shape(*right_theirs.shape)] + [shape(chunk + pairs, seqs)] * n_col,
        [((n_col, chunk, seqs), BF)],
    )
    lefts = spread(lefts, "col")
    rights = call(
        merge_right_kernel,
        "merge_right",
        (right_mine, partner(right_theirs, "seq", 1)),
        [shape(chunk + piece, seqs)] * n_row,
        [((n_row, piece, CZ), BF)],
    )
    rights = spread(rights, "row")
    pay, parts, pieces = call(
        functools.partial(weights_kernel, n_row, n_col),
        "weights",
        (normed, mask, *lefts[::-1], *rights[::-1]),
        (
            shape(4 * PROJ + piece, CZ),
            shape(q, 4 * PROJ, seqs),
            shape(n_col, pairs, CZ),
        ),
        [((chunk, seqs), F32)],
    )
    dx, token = call(
        input_kernel,
        "input",
        (flat, wl, wr, parts),
        (shape(seqs * q, ALIGN), shape(8, CZ, dtype=F32)),
        [((2, seqs * q, ALIGN // 2), F32)],
        cost=(2**28, 2**21),
    )
    increment, placed = call(
        functools.partial(place_kernel, q),
        "place",
        (pieces,),
        (shape(rows_i * rows_j, CZ), shape(8, CZ, dtype=F32)),
        cost=(2**20, 2**20),
    )

    (pay,) = call(
        functools.partial(sum_kernel, "col", n_col),
        "sum",
        (*sent_order(spread([pay] * n_col, "col")), token),
        (shape(*pay.shape),),
        [((n_col, *pay.shape), BF)],
    )
    (pay,) = call(
        functools.partial(join_kernel, "row", n_row),
        "join",
        (*spread([pay] * n_row, "row")[::-1], placed),
        (shape(4 * PROJ + n_row * piece, CZ),),
        [((n_row, 4 * PROJ, CZ), BF), ((n_row * piece, CZ), F32)],
    )
    d_first, d_second, d_couple = call(
        total_kernel,
        "total",
        (pay, partner(pay, "seq", 1)),
        (shape(PROJ, ALIGN, dtype=F32), shape(PROJ, ALIGN, dtype=F32), shape(OUTER, CZ, dtype=F32)),
    )
    return (
        increment.reshape(rows_i, rows_j, CZ),
        dx.reshape(seqs, q, ALIGN),
        d_first.T,
        d_second.T,
        d_couple,
    )


def solution(mesh):
    sizes = [mesh.shape[name] for name in AXES]
    placed = (
        P("seq", ("row", "col"), None),
        P(None, ("row", "col")),
        P(),
        P(),
        P(),
        P(("row", "seq"), "col", None),
    )
    return jax.shard_map(
        functools.partial(local, *sizes),
        mesh=mesh,
        in_specs=placed,
        out_specs=(P(("row", "seq"), "col", None), P("seq", ("row", "col"), None), P(), P(), P()),
        check_vma=False,
    )
```

```python
import functools
import math

import jax
import jax.numpy as jnp
from jax import lax
from jax.experimental import pallas as pl
from jax.experimental.pallas import tpu as pltpu
from jax.sharding import PartitionSpec as P

ALIGN = 256
PROJ = 32
CZ = 128
OUTER = 1024
PAD = 16
AXES = ("row", "col", "seq")
BF = jnp.bfloat16
F32 = jnp.float32

NN = (((1,), (0,)), ((), ()))
NT = (((1,), (1,)), ((), ()))
TN = (((0,), (0,)), ((), ()))


def dot(a, b, dims):
    return lax.dot_general(a, b, dims, preferred_element_type=F32)


def normalize(x):
    centered = x - jnp.mean(x, axis=-1, keepdims=True)
    rstd = lax.rsqrt(jnp.mean(centered * centered, axis=-1, keepdims=True) + 1e-05)
    return centered * rstd, rstd


def strided(ref, place):
    return jnp.concatenate([ref[0, place, :], ref[1, place, :]], axis=1)


def own_mask(mask_ref, seqs):
    start = pl.multiple_of(lax.axis_index("seq") * seqs, seqs)
    return mask_ref[:, pl.ds(start, seqs)].astype(F32)


def norm_kernel(x_ref, normed_ref, token_ref, rows):
    q, seqs, _ = normed_ref.shape
    xhat = normalize(x_ref[...].astype(F32))[0]
    rows[0], rows[1] = xhat[:, :128], xhat[:, 128:]
    for i in range(q):
        normed_ref[i] = strided(rows, pl.ds(i, seqs, stride=q)).astype(BF)
    token_ref[...] = jnp.zeros_like(token_ref)


def copy_all(pairs, sems):
    copies = [pltpu.make_async_copy(a, b, sems.at[k]) for k, (a, b) in enumerate(pairs)]
    for copy in copies:
        copy.start()
    return copies


def project_kernel(
    x_hbm, mask_hbm, wl_hbm, wr_hbm, adj_hbm,
    right_hbm, *refs
):
    *col_hbm, x_ref, mask_ref, wl_ref, wr_ref, adj_ref, right_ref, left_ref, pairs_ref, rows, spread, sems = refs
    q, seqs = mask_ref.shape[0], right_ref.shape[1]
    n_col = len(col_hbm)
    col = lax.axis_index("col")
    chunk = q * PROJ
    held = ((adj_hbm, adj_ref), (x_hbm, x_ref), (mask_hbm, mask_ref), (wl_hbm, wl_ref), (wr_hbm, wr_ref))
    loads = copy_all(held, sems)
    loads[0].wait()
    pairs = adj_ref[...].astype(F32).reshape(-1, n_col, q, CZ)
    for p in range(n_col):
        pairs_ref[p] = pairs[:, p].reshape(-1, CZ).astype(BF)
    place, rest = pl.ds(0, chunk + PAD), pl.ds(chunk + PAD, pairs_ref.shape[1])
    sent = copy_all(
        [(pairs_ref.at[col ^ k], hbm.at[rest, :]) for k, hbm in enumerate(col_hbm)],
        sems.at[pl.ds(6 + n_col, n_col)],
    )
    for copy in loads[1:]:
        copy.wait()
    xhat = normalize(x_ref[...].astype(F32))[0]
    rows[0], rows[1] = xhat[:, :128], xhat[:, 128:]
    mask = own_mask(mask_ref, seqs)
    weights = jnp.concatenate([wl_ref[...], wr_ref[...]], axis=0)
    for i in range(q):
        mine = strided(rows, pl.ds(i, seqs, stride=q)).astype(BF)
        both = dot(weights, mine, NT) * mask[i : i + 1, :]
        left_ref[i * PROJ : (i + 1) * PROJ, :] = both[:PROJ].astype(BF)
        spread[pl.ds(i, PROJ, stride=q), :] = both[PROJ:]
    whole = mask_ref[...].astype(F32)
    halves = [whole[:, t * seqs : (t + 1) * seqs] for t in range(whole.shape[1] // seqs)]
    tail = jnp.concatenate(halves, axis=0).astype(BF)
    left_ref[chunk:, :] = tail
    right_ref[...] = jnp.concatenate([spread[...].astype(BF), tail], axis=0)
    sent += copy_all(
        [(right_ref, right_hbm)]
        + [(left_ref, hbm.at[place, :]) for hbm in col_hbm],
        sems.at[pl.ds(5, n_col + 1)],
    )
    for copy in sent:
        copy.wait()


def far_first(count):
    return sorted(range(count), key=lambda k: (k & 2) == 0)


def by_partner(refs):
    return [refs[far_first(len(refs)).index(k)] for k in range(len(refs))]


def sent_order(values):
    return [values[k] for k in far_first(len(values))]


def unpack_mask(tail, q):
    tail = tail.astype(F32)
    return jnp.concatenate([tail[t * q : (t + 1) * q] for t in range(tail.shape[0] // q)], axis=1)


def pack_kernel(n_row, ready_ref, *refs):
    *ins, mine_ref, theirs_ref, mask_right, mask_left, adj_ref, left_ref, masks_ref = refs
    cols, rights = ins[:-n_row][::-1], ins[-n_row:]
    half, chunk = len(cols) // 2, mine_ref.shape[1]
    size, q = chunk + PAD, mask_right.shape[0] // n_row
    row, col, seq = (lax.axis_index(name) for name in AXES)
    for k, ref in enumerate(rights):
        mine_ref[row ^ k] = ref[:chunk, :]
        theirs_ref[row ^ k] = ref[:chunk, :]
        mask_right[pl.ds(pl.multiple_of((row ^ k) * q, q), q), :] = unpack_mask(ref[chunk:, :], q)
    for k, ref in enumerate(cols):
        left_ref[col ^ k] = ref[:chunk, :]
        masks_ref[col ^ k] = unpack_mask(ref[chunk:size, :], q)
        adj_ref[col ^ k] = ref[size:, :]
    for k in range(half):
        mine_ref[n_row + k] = left_ref[seq * half + k]
        theirs_ref[n_row + k] = left_ref[(1 - seq) * half + k]
        mask_left[k * q : (k + 1) * q, :] = masks_ref[seq * half + k]


def exchange(blocks):
    lane = lax.broadcasted_iota(jnp.int32, blocks[0].shape, 1)
    even = (lane & 32) == 0
    low = lane < 64
    a = list(blocks)
    for p in (0, 2):
        first, second = a[p], a[p + 1]
        a[p] = jnp.where(even, first, pltpu.roll(second, 32, 1))
        a[p + 1] = jnp.where(even, pltpu.roll(first, 96, 1), second)
    for p in (0, 1):
        first, second = a[p], a[p + 2]
        a[p] = jnp.where(low, first, pltpu.roll(second, 64, 1))
        a[p + 2] = jnp.where(low, pltpu.roll(first, 64, 1), second)
    return a


def back_kernel(
    wp, mr, ml, adj_ref, mine, dd, scaled_ref, recip_ref, rt_ref, d3
):
    n_col, pairs, _ = adj_ref.shape
    rows_i, depth = ml.shape
    rows_j, q = mr.shape[0], pairs // rows_i
    mask_r = mr[...]
    both = jnp.concatenate([(ml[i : i + 1, :] * mask_r).astype(BF) for i in range(rows_i)], axis=0)
    count = dot(both, jnp.ones((depth, CZ), BF), NN)
    recip = 1.0 / (count + 0.001)
    recip_ref[...] = recip
    adjoint = jnp.stack(
        [adj_ref[p].astype(F32).reshape(rows_i, q, CZ) for p in range(n_col)], axis=1
    ).reshape(rows_i * rows_j, CZ)
    scaled = (adjoint * recip).astype(BF)
    scaled_ref[...] = scaled.astype(F32).T.astype(BF)
    rt_ref[...] = by_channel(mine, mr.shape[0] // q, q)
    d3[...] = dot(scaled, wp[...], NT)
    for g in range(PROJ // 4):
        for ig in range(rows_i // 4):
            blocks = [
                d3[(ig * 4 + b) * rows_j : (ig * 4 + b + 1) * rows_j, g * 128 : (g + 1) * 128]
                for b in range(4)
            ]
            for e, value in enumerate(exchange(blocks)):
                row = (g * 4 + e) * rows_j
                dd[row : row + rows_j, ig * 128 : (ig + 1) * 128] = value.astype(BF)


def by_channel(packed, n_row, q):
    blocks = [packed[r].astype(F32).reshape(PROJ, q, -1) for r in range(n_row)]
    return jnp.concatenate(blocks, axis=1).reshape(PROJ * n_row * q, -1).astype(BF)


def left_kernel(rt_mine, theirs, dd, rt, mine_ref, theirs_ref, parts):
    half, chunk, seqs = mine_ref.shape
    n_row, q = theirs.shape[0] - half, chunk // PROJ
    seq = lax.axis_index("seq")
    rt[:, pl.ds(pl.multiple_of(seq * seqs, seqs), seqs)] = rt_mine[...]
    rt[:, pl.ds(pl.multiple_of((1 - seq) * seqs, seqs), seqs)] = by_channel(theirs, n_row, q)
    g_left = dot(dd[...], rt[...], TN)
    for t in range(2):
        for k in range(half):
            part = g_left[k * chunk : (k + 1) * chunk, t * seqs : (t + 1) * seqs]
            parts[t, k] = part.astype(BF)
    mine_ref[...] = parts[seq]
    theirs_ref[...] = parts[1 - seq]


def pair_kernel(
    rt, wp, dd, scaled_ref, recip_ref, mine, theirs,
    mine_ref, theirs_ref, couple_ref,
    lt, wf, o3, parts,
):
    n_col, pairs, _ = couple_ref.shape
    _, chunk, seqs = mine.shape
    q = chunk // PROJ
    half = n_col // 2
    rows_i = half * q
    rows_j = dd.shape[0] // PROJ
    n_row = rows_j // q
    depth = rt.shape[1]
    seq = lax.axis_index("seq")
    for ref, side in ((mine, seq), (theirs, 1 - seq)):
        lanes = pl.ds(pl.multiple_of(side * seqs, seqs), seqs)
        for k in range(half):
            lt[k * chunk : (k + 1) * chunk, lanes] = ref[n_row + k]
    for g in range(PROJ // 4):
        part = dot(rt[g * 4 * rows_j : (g + 1) * 4 * rows_j, :], lt[...], NT)
        for ig in range(rows_i // 4):
            lanes = slice(ig * 128, (ig + 1) * 128)
            blocks = [part[e * rows_j : (e + 1) * rows_j, lanes] for e in range(4)]
            for b, value in enumerate(exchange(blocks)):
                i = ig * 4 + b
                o3[i * rows_j : (i + 1) * rows_j, g * 128 : (g + 1) * 128] = value.astype(BF)
    couple = (dot(o3[...], wp[...], NN) * recip_ref[...]).reshape(rows_i, n_col, q, CZ)
    for p in range(n_col):
        couple_ref[p] = couple[:, p].reshape(pairs, CZ).astype(BF)
    dwo = dot(scaled_ref[...], o3[...], NN).T
    for e in range(PROJ):
        wf[pl.ds(e, PROJ, stride=PROJ), :] = dwo[e * PROJ : (e + 1) * PROJ, :]
    split = OUTER // 2 // chunk
    g_right = dot(dd[...], lt[...], NN).reshape(PROJ, rows_j, depth)
    for t in range(2):
        lanes = slice(t * seqs, (t + 1) * seqs)
        for r in range(n_row):
            parts[t, r] = g_right[:, r * q : (r + 1) * q, lanes].reshape(chunk, seqs).astype(BF)
        for k in range(split):
            row = (t * split + k) * chunk
            parts[t, n_row + k] = wf[row : row + chunk, :].astype(BF)
    mine_ref[...] = parts[seq]
    theirs_ref[...] = parts[1 - seq]


def merge_left_kernel(mine_ref, got_ref, couple_ref, held_ref, passed_ref, *refs):
    *outs, left_ref = refs
    passed_ref[...] = held_ref[...]
    half, chunk, _ = mine_ref.shape
    col, seq = lax.axis_index("col"), lax.axis_index("seq")
    for k in range(half):
        left_ref[seq * half + k] = mine_ref[k]
        left_ref[(1 - seq) * half + k] = got_ref[k]
    for k, ref in enumerate(outs):
        ref[:chunk, :] = left_ref[col ^ k]
        ref[chunk:, :] = couple_ref[col ^ k]


def merge_right_kernel(mine_ref, got_ref, *refs):
    *outs, dwo_ref = refs
    n_row, chunk = len(outs), mine_ref.shape[1]
    row = lax.axis_index("row")
    dwo = mine_ref[n_row:].astype(F32) + got_ref[n_row:].astype(F32)
    dwo_ref[...] = dwo.astype(BF).reshape(dwo_ref.shape)
    for k, ref in enumerate(outs):
        ref[:chunk, :] = (mine_ref[row ^ k].astype(F32) + got_ref[row ^ k].astype(F32)).astype(BF)
        ref[chunk:, :] = dwo_ref[row ^ k]


def add_all(refs):
    return functools.reduce(lambda a, b: a + b, [ref[...].astype(F32) for ref in refs])


def weights_kernel(n_row, n_col, normed_ref, mask_ref, *refs):
    col_refs, row_refs = refs[:n_col][::-1], refs[n_col : n_row + n_col][::-1]
    pay_ref, parts_ref, couple_ref, spread = refs[n_row + n_col :]
    q, seqs, _ = normed_ref.shape
    chunk = q * PROJ
    mask = own_mask(mask_ref, seqs)
    g_left = add_all([ref.at[:chunk, :] for ref in col_refs])
    g_right = add_all([ref.at[:chunk, :] for ref in row_refs])
    pay_ref[4 * PROJ :, :] = add_all([ref.at[chunk:, :] for ref in row_refs]).astype(BF)
    spread[...] = (g_right.reshape(PROJ, q, seqs) * mask[None]).reshape(chunk, seqs)
    total = jnp.zeros((4 * PROJ, ALIGN), F32)
    for i in range(q):
        left = g_left[i * PROJ : (i + 1) * PROJ] * mask[i : i + 1, :]
        g = jnp.concatenate([left, spread[pl.ds(i, PROJ, stride=q), :]], axis=0)
        high = g.astype(BF).astype(F32)
        parts = jnp.concatenate([high, g - high], axis=0).astype(BF)
        parts_ref[i] = parts
        total = total + dot(parts, normed_ref[i], NN)
    d_weights = total[: 2 * PROJ] + total[2 * PROJ :]
    pay_ref[: 2 * PROJ, :] = d_weights[:, :128].astype(BF)
    pay_ref[2 * PROJ : 4 * PROJ, :] = d_weights[:, 128:].astype(BF)
    for k, ref in enumerate(col_refs):
        couple_ref[lax.axis_index("col") ^ k] = ref[chunk:, :]


def hold_kernel(right_ref, left_ref, w_ref, right_out, left_out, wp_ref, wf):
    right_out[...] = right_ref[...]
    left_out[...] = left_ref[...]
    wf[...] = w_ref[...].astype(F32)
    for e in range(PROJ):
        wp_ref[e * PROJ : (e + 1) * PROJ, :] = wf[pl.ds(e, PROJ, stride=PROJ), :].astype(BF)


def input_kernel(x_ref, wl_ref, wr_ref, parts_ref, dx_ref, token_ref, rows):
    q, _, seqs = parts_ref.shape
    weights = jnp.concatenate([wl_ref[...], wr_ref[...]] * 2, axis=0)
    for i in range(q):
        d_rows = dot(parts_ref[i], weights, TN)
        rows[0, pl.ds(i, seqs, stride=q), :] = d_rows[:, :128]
        rows[1, pl.ds(i, seqs, stride=q), :] = d_rows[:, 128:]
    xhat, rstd = normalize(x_ref[...].astype(F32))
    d_normed = strided(rows, slice(None))
    along = jnp.mean(d_normed * xhat, axis=-1, keepdims=True)
    dx = rstd * (d_normed - jnp.mean(d_normed, axis=-1, keepdims=True) - xhat * along)
    dx_ref[...] = dx.astype(BF)
    token_ref[...] = jnp.zeros_like(token_ref)


def place_kernel(q, couple_ref, out_ref, token_ref):
    pieces = [couple_ref[p].astype(F32).reshape(-1, q, CZ) for p in range(couple_ref.shape[0])]
    out_ref[...] = jnp.stack(pieces, axis=1).reshape(-1, CZ).astype(BF)
    token_ref[...] = jnp.zeros_like(token_ref)


def sum_kernel(axis, size, *refs):
    out_ref, held = refs[-2:]
    for k, ref in enumerate(by_partner(refs[:size])):
        held[lax.axis_index(axis) ^ k] = ref[...]
    out_ref[...] = add_all([held.at[k] for k in range(size)]).astype(BF)


def join_kernel(axis, size, *refs):
    ins = refs[:size][::-1]
    out_ref, sums, runs = refs[-3:]
    head = 4 * PROJ
    rows = ins[0].shape[0] - head
    for k, ref in enumerate(ins):
        place = lax.axis_index(axis) ^ k
        sums[place] = ref[:head, :]
        runs[pl.ds(pl.multiple_of(place * rows, rows), rows), :] = ref[head:, :].astype(F32)
    out_ref[:head, :] = add_all([sums.at[k] for k in range(size)]).astype(BF)
    out_ref[head:, :] = runs[...].astype(BF)


def total_kernel(mine_ref, theirs_ref, first_ref, second_ref, dwo_ref):
    head = 4 * PROJ
    seq = lax.axis_index("seq")
    for ref, side in ((mine_ref, seq), (theirs_ref, 1 - seq)):
        start = pl.multiple_of(side * (OUTER // 2), OUTER // 2)
        dwo_ref[pl.ds(start, OUTER // 2), :] = ref[head:, :].astype(F32)
    total = mine_ref[:head, :].astype(F32) + theirs_ref[:head, :].astype(F32)
    first_ref[:, :128] = total[:PROJ]
    first_ref[:, 128:] = total[2 * PROJ : 3 * PROJ]
    second_ref[:, :128] = total[PROJ : 2 * PROJ]
    second_ref[:, 128:] = total[3 * PROJ :]


def params(mib):
    return pltpu.CompilerParams(vmem_limit_bytes=mib * 1024 * 1024)


def shape(*dims, dtype=BF):
    return jax.ShapeDtypeStruct(dims, dtype)


def call(kernel, name, inputs, outputs, scratch=(), hbm_in=0, hbm_out=0, sems=0, mib=None, cost=None):
    def specs(count, hbm):
        return [pl.BlockSpec(memory_space=pltpu.HBM if k < hbm else pltpu.VMEM) for k in range(count)]

    held = sum(2 * math.prod(dims) for dims, _ in scratch)
    buffers = [pltpu.VMEM(dims, dtype) for dims, dtype in scratch]
    if sems:
        buffers.append(pltpu.SemaphoreType.DMA((sems,)))
    return pl.pallas_call(
        kernel,
        out_shape=outputs,
        in_specs=specs(len(inputs), hbm_in),
        out_specs=tuple(specs(len(outputs), hbm_out)),
        scratch_shapes=buffers,
        compiler_params=params(mib or 16 + 2 * held // 1024**2),
        cost_estimate=cost and pl.CostEstimate(flops=cost[0], bytes_accessed=cost[1], transcendentals=0),
        name=name,
    )(*inputs)


def local(n_row, n_col, n_seq, x, occupancy, first, second, couple, adjoint):
    seqs, q, _ = x.shape
    rows_i, rows_j, _ = adjoint.shape
    half = n_col // n_seq
    chunk = q * PROJ
    depth = seqs * n_seq
    pairs = rows_i * q
    flat = x.reshape(seqs * q, ALIGN)
    mask = occupancy.T
    wl, wr = first.T, second.T

    right, *lefts = call(
        project_kernel,
        "project",
        (flat, mask, wl, wr, adjoint.reshape(rows_i * rows_j, CZ)),
        (
            shape(chunk + PAD, seqs),
            *[shape(chunk + PAD + pairs, seqs)] * n_col,
        ),
        [
            ((seqs * q, ALIGN), BF),
            ((q, depth), jnp.int32),
            ((PROJ, ALIGN), BF),
            ((PROJ, ALIGN), BF),
            ((rows_i * rows_j, CZ), BF),
            ((chunk + PAD, seqs), BF),
            ((chunk + PAD, seqs), BF),
            ((n_col, pairs, CZ), BF),
            ((2, seqs * q, ALIGN // 2), F32),
            ((chunk, seqs), F32),
        ],
        hbm_in=5,
        hbm_out=1 + n_col,
        sems=6 + 2 * n_col,
        mib=60,
    )

    def partner(value, axis, k):
        size = {"row": n_row, "col": n_col, "seq": n_seq}[axis]
        return lax.ppermute(value, axis, [(d, d ^ k) for d in range(size)])

    def spread(values, axis):
        return [values[0]] + [partner(values[k], axis, k) for k in range(1, len(values))]

    held, left, wp = call(
        hold_kernel,
        "hold",
        (right, lefts[0], couple),
        (shape(*right.shape), shape(*lefts[0].shape), shape(OUTER, CZ)),
        [((OUTER, CZ), F32)],
        cost=(2**20, 2**20),
    )
    rights = [held] + spread([right] * n_row, "row")[1:]
    lefts = [left] + spread(lefts, "col")[1:]
    normed, ready = call(
        norm_kernel,
        "norm",
        (flat,),
        (shape(q, seqs, ALIGN), shape(8, CZ, dtype=F32)),
        [((2, seqs * q, ALIGN // 2), F32)],
        cost=(2**28, 2**21),
    )
    count = n_row + half
    mine, theirs, mask_right, mask_left, adjoints = call(
        functools.partial(pack_kernel, n_row),
        "pack",
        (ready, *lefts[::-1], *rights),
        (
            shape(count, chunk, seqs),
            shape(count, chunk, seqs),
            shape(rows_j, depth, dtype=F32),
            shape(rows_i, depth, dtype=F32),
            shape(n_col, pairs, CZ),
        ),
        [((n_col, chunk, seqs), BF), ((n_col, q, depth), F32)],
    )
    theirs = partner(theirs, "seq", 1)
    dd, scaled, recip, rt_mine = call(
        back_kernel,
        "back",
        (wp, mask_right, mask_left, adjoints, mine),
        (
            shape(PROJ * rows_j, rows_i * PROJ),
            shape(CZ, rows_i * rows_j),
            shape(rows_i * rows_j, CZ, dtype=F32),
            shape(PROJ * rows_j, seqs),
        ),
        [((rows_i * rows_j, OUTER), F32)],
        cost=(2**30, 2**23),
    )
    rt, left_mine, left_theirs = call(
        left_kernel,
        "left",
        (rt_mine, theirs, dd),
        (shape(PROJ * rows_j, depth), shape(half, chunk, seqs), shape(half, chunk, seqs)),
        [((2, half, chunk, seqs), BF)],
        cost=(2**30, 2**23),
    )
    got = partner(left_theirs, "seq", 1)
    parts = n_row + OUTER // 2 // chunk
    right_mine, right_theirs, pieces = call(
        pair_kernel,
        "pair",
        (rt, wp, dd, scaled, recip, mine, theirs),
        (
            shape(parts, chunk, seqs),
            shape(parts, chunk, seqs),
            shape(n_col, pairs, CZ),
        ),
        [
            ((rows_i * PROJ, depth), BF),
            ((OUTER, CZ), F32),
            ((rows_i * rows_j, OUTER), BF),
            ((2, parts, chunk, seqs), BF),
        ],
        cost=(2**30, 2**23),
    )
    piece = OUTER // 2 // n_row
    right_theirs, *lefts = call(
        merge_left_kernel,
        "merge_left",
        (left_mine, got, pieces, right_theirs),
        [shape(*right_theirs.shape)] + [shape(chunk + pairs, seqs)] * n_col,
        [((n_col, chunk, seqs), BF)],
    )
    lefts = spread(lefts, "col")
    rights = call(
        merge_right_kernel,
        "merge_right",
        (right_mine, partner(right_theirs, "seq", 1)),
        [shape(chunk + piece, seqs)] * n_row,
        [((n_row, piece, CZ), BF)],
    )
    rights = spread(rights, "row")
    order = sorted(range(n_row), key=lambda k: -bin(k).count("1"))
    pay, parts, pieces = call(
        functools.partial(weights_kernel, n_row, n_col),
        "weights",
        (normed, mask, *lefts[::-1], *[rights[k] for k in order]),
        (
            shape(4 * PROJ + piece, CZ),
            shape(q, 4 * PROJ, seqs),
            shape(n_col, pairs, CZ),
        ),
        [((chunk, seqs), F32)],
    )
    dx, token = call(
        input_kernel,
        "input",
        (flat, wl, wr, parts),
        (shape(seqs * q, ALIGN), shape(8, CZ, dtype=F32)),
        [((2, seqs * q, ALIGN // 2), F32)],
        cost=(2**28, 2**21),
    )
    increment, placed = call(
        functools.partial(place_kernel, q),
        "place",
        (pieces,),
        (shape(rows_i * rows_j, CZ), shape(8, CZ, dtype=F32)),
        cost=(2**20, 2**20),
    )

    (pay,) = call(
        functools.partial(sum_kernel, "col", n_col),
        "sum",
        (*sent_order(spread([pay] * n_col, "col")), token),
        (shape(*pay.shape),),
        [((n_col, *pay.shape), BF)],
    )
    (pay,) = call(
        functools.partial(join_kernel, "row", n_row),
        "join",
        (*spread([pay] * n_row, "row")[::-1], placed),
        (shape(4 * PROJ + n_row * piece, CZ),),
        [((n_row, 4 * PROJ, CZ), BF), ((n_row * piece, CZ), F32)],
    )
    d_first, d_second, d_couple = call(
        total_kernel,
        "total",
        (pay, partner(pay, "seq", 1)),
        (shape(PROJ, ALIGN, dtype=F32), shape(PROJ, ALIGN, dtype=F32), shape(OUTER, CZ, dtype=F32)),
    )
    return (
        increment.reshape(rows_i, rows_j, CZ),
        dx.reshape(seqs, q, ALIGN),
        d_first.T,
        d_second.T,
        d_couple,
    )


def solution(mesh):
    sizes = [mesh.shape[name] for name in AXES]
    placed = (
        P("seq", ("row", "col"), None),
        P(None, ("row", "col")),
        P(),
        P(),
        P(),
        P(("row", "seq"), "col", None),
    )
    return jax.shard_map(
        functools.partial(local, *sizes),
        mesh=mesh,
        in_specs=placed,
        out_specs=(P(("row", "seq"), "col", None), P("seq", ("row", "col"), None), P(), P(), P()),
        check_vma=False,
    )
```
